32 devices in a mesh: ctx: 4 (over y, x), head: 8 (over z, core).
Axes of the slice: x: 2, y: 2, z: 4, core: 2. Of those that a mesh axis runs over, the one named last changes fastest.
Arguments:
- queries: bfloat16 [256, 16384], P(None, 'head'), may hold values from -64 to 64, as said below
- grad_out: bfloat16 [256, 16384], P(None, 'head'), may hold values from -24 to 24
- latent: bfloat16 [8192, 512], P(('ctx', 'head')), may hold values from -6.1 to 6.1
- up_key: bfloat16 [512, 16384], P(None, 'head'), as said below
- up_value: bfloat16 [512, 16384], P(None, 'head'), may hold values from -0.25 to 0.25
Outputs:
- grad_queries: float32 [256, 16384], P('ctx', 'head')
- grad_latent: float32 [8192, 512], P(('ctx', 'head'))
- grad_up_key: float32 [512, 16384], P('ctx', 'head')
- grad_up_value: float32 [512, 16384], P('ctx', 'head')
The draws below stay inside these ranges and needn't reach their ends.
Inputs may be any that keep to these rules, and one draw needn't show every extreme that they name: `queries`: entries lie within 64 in magnitude. `up_key`: entries lie within 4 / sqrt(512) in magnitude.
All inputs are finite; a program needn't handle non-finite values.
Results may differ from the reference program's by a relative error of at most 0.005.
Values may be sent and summed in bfloat16 or wider, within the bound.
No kernel may reach another device: no remote copies, remote signals or barrier semaphores. Data moves between devices by JAX's collectives and lax.ppermute only.
A program may use at most 128 MiB of HBM per device.

```python
import math
import jax
import jax.numpy as jnp
from jax import lax

HEADS = 128
HD = 128
LATENT = 512
QTOK = 256
CTX_LEN = 8192


def shared_arrays(key):
    base = jax.random.fold_in(key, 7001)
    normal = jnp.clip(jax.random.normal(jax.random.fold_in(base, 1), (CTX_LEN, LATENT), jnp.float32), -4.0, 4.0)
    rising = 0.6 + 0.7 * jnp.arange(CTX_LEN, dtype=jnp.float32) / CTX_LEN
    jitter = jnp.exp(jax.random.uniform(jax.random.fold_in(base, 2), (CTX_LEN, 1), jnp.float32, -0.15, 0.15))
    latent = normal * rising[:, None] * jitter
    up_key = jnp.clip(jax.random.normal(jax.random.fold_in(base, 3), (LATENT, HEADS * HD), jnp.float32), -4.0, 4.0) / math.sqrt(LATENT)
    return (latent, up_key)


def draw_latent(key, part):
    return shared_arrays(key)[0].astype(jnp.bfloat16)


def draw_up_key(key, part):
    return shared_arrays(key)[1].astype(jnp.bfloat16)


def draw_queries(key, part):
    drawn = jnp.clip(jax.random.normal(jax.random.fold_in(key, 41), (QTOK, HEADS * HD), jnp.float32), -4.0, 4.0)
    return jnp.clip(drawn, -64.0, 64.0).astype(jnp.bfloat16)


def shard_levels(stream_key, extent, cuts, low, top_value):
    gain, own = 1.0, jax.random.fold_in(stream_key, 6)
    for dim, parts in cuts:
        steps = jnp.exp(jax.random.uniform(jax.random.fold_in(own, dim), (parts,), jnp.float32, low / len(cuts), top_value / len(cuts)))
        gain = gain * jnp.repeat(steps, extent[dim] // parts).reshape([-1 if axis == dim else 1 for axis in range(len(extent))])
    return gain


def normal_values(own_key, extent, width, bound, split=(), kind=jnp.bfloat16):
    result = jax.random.normal(own_key, extent, jnp.float32) * width
    if len(split) > 0:
        result = shard_levels(own_key, extent, split, -0.22, 0.18) * result
    return jnp.clip(result, min=-bound, max=bound).astype(kind)


def setup_inputs(seed: int = 0) -> dict:
    arg_keys = jax.random.split(jax.random.key(seed), 6)
    return {
        "queries": draw_queries(jax.random.fold_in(arg_keys[5], 71), 0),
        "grad_out": normal_values(arg_keys[1], (QTOK, HEADS * HD), 4.0, 24.0, ((1, 8),)),
        "latent": draw_latent(jax.random.fold_in(arg_keys[5], 71), 0),
        "up_key": draw_up_key(jax.random.fold_in(arg_keys[5], 71), 0),
        "up_value": normal_values(arg_keys[4], (LATENT, HEADS * HD), LATENT ** -0.5, 0.25, ((1, 8),)),
    }


def reference(queries, grad_out, latent, up_key, up_value):
    scale = 1.0 / math.sqrt(HD)
    query_pos = CTX_LEN - QTOK + jnp.arange(QTOK, dtype=jnp.int32)
    key_pos = jnp.arange(CTX_LEN, dtype=jnp.int32)
    visible = key_pos[None, :] <= query_pos[:, None]

    def one_head(carry, head_index):
        offset = head_index * HD
        query_head = lax.dynamic_slice_in_dim(queries, offset, HD, 1)
        grad_head = lax.dynamic_slice_in_dim(grad_out, offset, HD, 1)
        key_weight = lax.dynamic_slice_in_dim(up_key, offset, HD, 1)
        value_weight = lax.dynamic_slice_in_dim(up_value, offset, HD, 1)
        key_head = jnp.dot(latent, key_weight, preferred_element_type=jnp.float32)
        value_head = jnp.dot(latent, value_weight, preferred_element_type=jnp.float32).astype(jnp.bfloat16)
        raw = jnp.dot(query_head.astype(jnp.float32), key_head.T, precision=lax.Precision.HIGHEST) * scale
        scores = jnp.where(visible, raw, -jnp.inf)
        maxima = lax.optimization_barrier(jnp.max(scores, axis=1))
        weights = jnp.exp(scores - maxima[:, None])
        totals = lax.optimization_barrier(jnp.sum(weights, axis=1))
        probs = weights / totals[:, None]
        grad_probs = jnp.dot(grad_head, value_head.T, preferred_element_type=jnp.float32)
        deltas = lax.optimization_barrier(jnp.sum(probs * grad_probs, axis=1))
        grad_scores = (probs * (grad_probs - deltas[:, None]) * scale).astype(jnp.bfloat16)
        query_grad = jnp.dot(grad_scores.astype(jnp.float32), key_head, precision=lax.Precision.HIGHEST)
        key_grad = jnp.dot(grad_scores.T, query_head, preferred_element_type=jnp.float32).astype(jnp.bfloat16)
        value_grad = jnp.dot(probs.astype(jnp.bfloat16).T, grad_head, preferred_element_type=jnp.float32).astype(jnp.bfloat16)
        latent_part = jnp.dot(key_grad, key_weight.T, preferred_element_type=jnp.float32) + jnp.dot(value_grad, value_weight.T, preferred_element_type=jnp.float32)
        key_weight_grad = jnp.dot(latent.T, key_grad, preferred_element_type=jnp.float32)
        value_weight_grad = jnp.dot(latent.T, value_grad, preferred_element_type=jnp.float32)
        return (carry + latent_part, (query_grad, key_weight_grad, value_weight_grad))
    initial = jnp.zeros((CTX_LEN, LATENT), jnp.float32)
    grad_latent, stacked = lax.scan(one_head, initial, jnp.arange(HEADS, dtype=jnp.int32))
    grad_queries = jnp.transpose(stacked[0], (1, 0, 2)).reshape(QTOK, HEADS * HD)
    grad_up_key = jnp.transpose(stacked[1], (1, 0, 2)).reshape(LATENT, HEADS * HD)
    grad_up_value = jnp.transpose(stacked[2], (1, 0, 2)).reshape(LATENT, HEADS * HD)
    return (grad_queries, grad_latent, grad_up_key, grad_up_value)
```

```python
import functools
import math

import jax
import jax.numpy as jnp
from jax import lax
from jax.experimental import pallas as pl
from jax.experimental.pallas import tpu as pltpu
from jax.sharding import PartitionSpec as P

HD = 128
GROUPS = 4
PAIR = 2
VMEM = 60 << 20
NT = (((1,), (1,)), ((), ()))
TN = (((0,), (0,)), ((), ()))
NN = (((1,), (0,)), ((), ()))
SCALE = 1.0 / math.sqrt(HD)
LOG2E = math.log2(math.e)
F32 = jnp.float32
BF16 = jnp.bfloat16


def dot(a, b, dims=NN):
    return lax.dot_general(a, b, dims, preferred_element_type=F32)


def swap(array, axis, distance):
    count = lax.axis_size(axis)
    return lax.ppermute(array, axis, [(i, i ^ distance) for i in range(count)])


def masked(s, gap):
    rows = lax.broadcasted_iota(jnp.int32, s.shape, 0)
    cols = lax.broadcasted_iota(jnp.int32, s.shape, 1)
    return jnp.where(rows - cols > gap, -jnp.inf, s)


def lanes(head):
    return slice(head * HD, (head + 1) * HD)


def join(parts):
    m = functools.reduce(jnp.maximum, [p[0] for p in parts])
    factors = [jnp.exp2(p[0] - m) for p in parts]
    t = sum(p[1] * f for p, f in zip(parts, factors))
    d = sum(p[2] * f for p, f in zip(parts, factors))
    return m, t, d


def triple(ref, head):
    return tuple(ref[3 * head + i : 3 * head + i + 1, :] for i in range(3))


def stats_kernel(chunk, gaps_ref, a_ref, b_ref, uk_ref, uv_ref, q_ref, do_ref, *refs):
    k2_ref, v_ref, latt_ref, st_ref = refs[-4:]
    rb = a_ref.shape[0]
    qn = q_ref.shape[0]
    pair = range(PAIR)
    weights = [jnp.concatenate([uk_ref[:, lanes(a)], uv_ref[:, lanes(a)]], axis=1) for a in pair]
    q = [q_ref[:, lanes(a)] for a in pair]
    qq = [jnp.concatenate([x, x], axis=1) for x in q]
    do = [do_ref[:, lanes(a)] for a in pair]
    parts = [[] if chunk == 0 else [triple(refs[0], a)] for a in pair]
    for side, lat_ref in enumerate((a_ref, b_ref)):
        rows = pl.ds(side * rb, rb)
        for a in pair:
            kv = dot(lat_ref[...], weights[a])
            k = kv[:, :HD] * (SCALE * LOG2E)
            hi = k.astype(BF16)
            lo = (k - hi.astype(F32)).astype(BF16)
            k2 = jnp.concatenate([hi, lo], axis=1)
            v = kv[:, HD:].astype(BF16)
            k2_ref[a, rows, :] = k2
            v_ref[a, rows, :] = v
            s = masked(dot(k2, qq[a], NT), gaps_ref[2 * chunk + side])
            gp = dot(v, do[a], NT)
            m = jnp.maximum(jnp.max(s, axis=0, keepdims=True), -1e30)
            w = jnp.exp2(s - m)
            parts[a].append((m, jnp.sum(w, axis=0, keepdims=True), jnp.sum(w * gp, axis=0, keepdims=True)))
    pad = jnp.zeros((8 - 3 * PAIR, qn), F32)
    st_ref[...] = jnp.concatenate([x for a in pair for x in join(parts[a])] + [pad], axis=0)

    @pl.when(pl.program_id(0) == 0)
    def _():
        latt_ref[:, 0:rb] = a_ref[...].T
        latt_ref[:, rb : 2 * rb] = b_ref[...].T


def run_stats(chunk, gaps, a, b, up_key, up_value, queries, grad_out, before):
    rb, depth = a.shape
    heads = queries.shape[1] // HD
    qn = queries.shape[0]
    wide = PAIR * HD
    col = lambda g, *_: (0, g)
    whole = pl.BlockSpec((rb, depth), lambda g, *_: (0, 0))
    st_spec = pl.BlockSpec((None, 8, qn), lambda g, *_: (g, 0, 0))
    extra = () if before is None else (before,)
    return pl.pallas_call(
        functools.partial(stats_kernel, chunk),
        out_shape=(
            jax.ShapeDtypeStruct((heads, 2 * rb, 2 * HD), BF16),
            jax.ShapeDtypeStruct((heads, 2 * rb, HD), BF16),
            jax.ShapeDtypeStruct((depth, 2 * rb), BF16),
            jax.ShapeDtypeStruct((heads // PAIR, 8, qn), F32),
        ),
        grid_spec=pltpu.PrefetchScalarGridSpec(
            num_scalar_prefetch=1,
            grid=(heads // PAIR,),
            in_specs=[
                whole,
                whole,
                pl.BlockSpec((depth, wide), col),
                pl.BlockSpec((depth, wide), col),
                pl.BlockSpec((qn, wide), col),
                pl.BlockSpec((qn, wide), col),
            ]
            + [st_spec] * len(extra),
            out_specs=[
                pl.BlockSpec((PAIR, 2 * rb, 2 * HD), lambda g, *_: (g, 0, 0)),
                pl.BlockSpec((PAIR, 2 * rb, HD), lambda g, *_: (g, 0, 0)),
                pl.BlockSpec((depth, 2 * rb), lambda g, *_: (0, 0)),
                st_spec,
            ],
        ),
        compiler_params=pltpu.CompilerParams(vmem_limit_bytes=VMEM),
        cost_estimate=pl.CostEstimate(
            flops=heads * 2 * rb * HD * 2 * (2 * depth + 4 * qn),
            bytes_accessed=heads * 2 * rb * HD * 6,
            transcendentals=heads * 2 * rb * qn,
        ),
        name="stats",
    )(gaps, a, b, up_key, up_value, queries, grad_out, *extra)


def grads_kernel(n, chunks, gaps_ref, q_ref, do_ref, st_ref, *refs):
    k2_refs, v_refs = refs[:chunks], refs[chunks : 2 * chunks]
    gk_ref, gv_ref, gq_ref = refs[2 * chunks :]
    rows2 = k2_refs[0].shape[1]
    rb = rows2 // 2
    qn = q_ref.shape[0]
    pair = range(PAIR)
    q = [q_ref[:, lanes(a)] for a in pair]
    qq = [jnp.concatenate([x, x], axis=1) for x in q]
    do = [do_ref[:, lanes(a)] for a in pair]
    shift, delta = [], []
    for a in pair:
        m, t, d = join([triple(st_ref.at[i], a) for i in range(n)])
        shift.append(m + jnp.log2(t))
        delta.append(d / t)
    gq = [jnp.zeros((qn, 2 * HD), F32) for a in pair]
    for c in range(chunks):
        rows = pl.ds(c * rows2, rows2)
        for a in pair:
            k2 = k2_refs[c][a]
            s = dot(k2, qq[a], NT)
            s = jnp.concatenate([masked(s[:rb], gaps_ref[2 * c]), masked(s[rb:], gaps_ref[2 * c + 1])], axis=0)
            gp = dot(v_refs[c][a], do[a], NT)
            p = jnp.exp2(s - shift[a])
            ds = (p * (gp - delta[a]) * SCALE).astype(BF16)
            low = p.astype(BF16)
            gk_ref[rows, lanes(a)] = dot(ds, q[a]).astype(BF16)
            gv_ref[rows, lanes(a)] = dot(low, do[a]).astype(BF16)
            gq[a] = gq[a] + dot(ds, k2, TN)
    for a in pair:
        gq_ref[:, lanes(a)] = (gq[a][:, :HD] + gq[a][:, HD:]) * (1.0 / (SCALE * LOG2E))


def run_grads(gaps, queries, grad_out, k2, v, stats, first_head, per):
    chunks = len(k2)
    n = stats.shape[0]
    rows2 = k2[0].shape[1]
    rows = chunks * rows2
    qn = queries.shape[0]
    wide = PAIR * HD
    base = first_head // PAIR
    col = lambda g, *_: (0, base + g)
    out = lambda g, *_: (0, g)
    return pl.pallas_call(
        functools.partial(grads_kernel, n, chunks),
        out_shape=(
            jax.ShapeDtypeStruct((rows, per * HD), BF16),
            jax.ShapeDtypeStruct((rows, per * HD), BF16),
            jax.ShapeDtypeStruct((qn, per * HD), F32),
        ),
        grid_spec=pltpu.PrefetchScalarGridSpec(
            num_scalar_prefetch=1,
            grid=(per // PAIR,),
            in_specs=[
                pl.BlockSpec((qn, wide), col),
                pl.BlockSpec((qn, wide), col),
                pl.BlockSpec((n, None, 8, qn), lambda g, *_: (0, base + g, 0, 0)),
            ]
            + [pl.BlockSpec((PAIR, rows2, 2 * HD), lambda g, *_: (base + g, 0, 0))] * chunks
            + [pl.BlockSpec((PAIR, rows2, HD), lambda g, *_: (base + g, 0, 0))] * chunks,
            out_specs=[
                pl.BlockSpec((rows, wide), out),
                pl.BlockSpec((rows, wide), out),
                pl.BlockSpec((qn, wide), out),
            ],
        ),
        compiler_params=pltpu.CompilerParams(vmem_limit_bytes=VMEM),
        cost_estimate=pl.CostEstimate(
            flops=per * rows * HD * 2 * 7 * qn,
            bytes_accessed=per * rows * HD * 10,
            transcendentals=per * rows * qn,
        ),
        name="grads",
    )(gaps, queries, grad_out, stats, *k2, *v)


def ups_kernel(n, chunks, gk_ref, gv_ref, gq_ref, *refs):
    latt_refs, out_ref = refs[:chunks], refs[chunks]
    step = pl.program_id(0)
    depth, rows2 = latt_refs[0].shape
    rb, qb = depth // n, gq_ref.shape[0] // n
    wide = gk_ref.shape[1]
    half = out_ref.shape[2] // 2
    for side, ref in enumerate((gk_ref, gv_ref)):
        cols = pl.ds(pl.multiple_of(side * half + step * wide, wide), wide)
        gu = sum(dot(latt_refs[c][...], ref[pl.ds(c * rows2, rows2), :]) for c in range(chunks))
        for r in range(n):
            out_ref[r, 0:rb, cols] = gu[r * rb : (r + 1) * rb].astype(BF16)
            part = pl.ds(r * qb + side * (qb // 2), qb // 2)
            out_ref[r, rb : rb + qb // 2, cols] = gq_ref[part, :].astype(BF16)


def run_ups(n, latt, gk, gv, gq):
    chunks = len(latt)
    depth, rows2 = latt[0].shape
    rows, cols = gk.shape
    qn = gq.shape[0]
    wide = PAIR * HD
    shape = (n, depth // n + qn // n // 2, 2 * cols)
    block = lambda g: (0, g)
    return pl.pallas_call(
        functools.partial(ups_kernel, n, chunks),
        out_shape=jax.ShapeDtypeStruct(shape, BF16),
        grid=(cols // wide,),
        in_specs=[
            pl.BlockSpec((rows, wide), block),
            pl.BlockSpec((rows, wide), block),
            pl.BlockSpec((qn, wide), block),
        ]
        + [pl.BlockSpec((depth, rows2), lambda g: (0, 0))] * chunks,
        out_specs=pl.BlockSpec(shape, lambda g: (0, 0, 0)),
        compiler_params=pltpu.CompilerParams(vmem_limit_bytes=VMEM),
        cost_estimate=pl.CostEstimate(
            flops=4 * depth * rows * cols, bytes_accessed=4 * rows * cols, transcendentals=0
        ),
        name="ups",
    )(gk, gv, gq, *latt)


def latent_kernel(groups, uk_ref, uv_ref, *refs):
    keep_ref, send_ref = refs[-2:]
    per = refs[0].shape[1]
    total = None
    for g in range(groups):
        for w_ref, ref in ((uk_ref, refs[2 * g]), (uv_ref, refs[2 * g + 1])):
            term = dot(ref[...], w_ref[:, g * per : (g + 1) * per], NT)
            total = term if total is None else total + term
    rb = keep_ref.shape[0]
    keep_ref[...] = total[:rb].astype(BF16)
    send_ref[...] = total[rb:].astype(BF16)


def run_latent(up_key, up_value, gkv, rb):
    depth, width = up_key.shape
    rows, per = gkv[0].shape
    steps = rows // (2 * rb)
    whole = pl.BlockSpec((depth, width), lambda i: (0, 0))
    out = jax.ShapeDtypeStruct((steps, rb, depth), BF16)
    out_spec = pl.BlockSpec((None, rb, depth), lambda i: (i, 0, 0))
    return pl.pallas_call(
        functools.partial(latent_kernel, len(gkv) // 2),
        out_shape=(out, out),
        grid=(steps,),
        in_specs=[whole, whole] + [pl.BlockSpec((2 * rb, per), lambda i: (i, 0))] * len(gkv),
        out_specs=[out_spec, out_spec],
        compiler_params=pltpu.CompilerParams(vmem_limit_bytes=VMEM),
        cost_estimate=pl.CostEstimate(
            flops=4 * rows * depth * width, bytes_accessed=4 * rows * width, transcendentals=0
        ),
        name="latents",
    )(up_key, up_value, *gkv)


def local(queries, grad_out, latent, up_key, up_value):
    heads = queries.shape[1] // HD
    qn = queries.shape[0]
    n = lax.axis_size("ctx")
    mates = lax.axis_size("head")
    rb, depth = latent.shape
    chunks = mates // 2

    firsts = [latent] + [swap(latent, "head", 2 * k) for k in range(1, chunks)]
    seconds = [swap(x, "head", 1) for x in firsts]
    starts = (lax.axis_index("ctx") * mates + (lax.axis_index("head") ^ jnp.arange(mates))) * rb
    gaps = (rb * mates * n - qn - starts).astype(jnp.int32)
    k2, v, latt, stats = [], [], [], None
    for c in range(chunks):
        one_k2, one_v, one_latt, stats = run_stats(
            c, gaps, firsts[c], seconds[c], up_key, up_value, queries, grad_out, stats
        )
        k2.append(one_k2)
        v.append(one_v)
        latt.append(one_latt)
    stats = jnp.stack([stats] + [swap(stats, "ctx", k) for k in range(1, n)])

    per = heads // GROUPS
    gkv, gqs, outs = [], [], []

    def send(g):
        part = run_ups(n, latt, gkv[2 * g], gkv[2 * g + 1], gqs[g])
        outs.append(lax.all_to_all(part, "ctx", 0, 0, tiled=True))

    for g in range(GROUPS):
        gk, gv, gq = run_grads(gaps, queries, grad_out, k2, v, stats, g * per, per)
        gkv += [gk, gv]
        gqs.append(gq)
        if g < GROUPS // 2:
            send(g)
    keep, away = run_latent(up_key, up_value, gkv, rb)
    for g in range(GROUPS // 2, GROUPS):
        send(g)
    both = keep.astype(F32) + swap(away, "head", 1).astype(F32)
    low = both.astype(BF16)
    grad_latent = both[0]
    for k in range(1, chunks):
        grad_latent = grad_latent + swap(low[k], "head", 2 * k).astype(F32)

    sums = [jnp.sum(o.astype(F32), axis=0) for o in outs]
    ub = depth // n
    cols = per * HD
    grad_key = jnp.concatenate([s[:ub, :cols] for s in sums], axis=1)
    grad_value = jnp.concatenate([s[:ub, cols:] for s in sums], axis=1)
    grad_q = jnp.concatenate([jnp.concatenate([s[ub:, :cols], s[ub:, cols:]], axis=0) for s in sums], axis=1)
    return (grad_q, grad_latent, grad_key, grad_value)


def solution(mesh):
    return jax.shard_map(
        local,
        mesh=mesh,
        in_specs=(
            P(None, "head"),
            P(None, "head"),
            P(("ctx", "head"), None),
            P(None, "head"),
            P(None, "head"),
        ),
        out_specs=(P("ctx", "head"), P(("ctx", "head"), None), P("ctx", "head"), P("ctx", "head")),
        check_vma=False,
    )
```

```python
import functools
import math

import jax
import jax.numpy as jnp
from jax import lax
from jax.experimental import pallas as pl
from jax.experimental.pallas import tpu as pltpu
from jax.sharding import PartitionSpec as P

HD = 128
PAIR = 2
WIDE = 4
VMEM = 60 << 20
NT = (((1,), (1,)), ((), ()))
TN = (((0,), (0,)), ((), ()))
NN = (((1,), (0,)), ((), ()))
SCALE = 1.0 / math.sqrt(HD)
LOG2E = math.log2(math.e)
F32 = jnp.float32
BF16 = jnp.bfloat16


def dot(a, b, dims=NN):
    return lax.dot_general(a, b, dims, preferred_element_type=F32)


def swap(array, axis, distance):
    count = lax.axis_size(axis)
    return lax.ppermute(array, axis, [(i, i ^ distance) for i in range(count)])


def masked(s, gap):
    rows = lax.broadcasted_iota(jnp.int32, s.shape, 0)
    cols = lax.broadcasted_iota(jnp.int32, s.shape, 1)
    return jnp.where(rows - cols > gap, -jnp.inf, s)


def lanes(head):
    return slice(head * HD, (head + 1) * HD)


def join(parts):
    m = functools.reduce(jnp.maximum, [p[0] for p in parts])
    factors = [jnp.exp2(p[0] - m) for p in parts]
    t = sum(p[1] * f for p, f in zip(parts, factors))
    d = sum(p[2] * f for p, f in zip(parts, factors))
    return m, t, d


def triple(ref, head):
    return tuple(ref[3 * head + i : 3 * head + i + 1, :] for i in range(3))


def stats_kernel(first, pieces, gaps_ref, uk_ref, uv_ref, q_ref, do_ref, *refs):
    lat_refs = refs[:pieces]
    k2_ref, v_ref, st_ref = refs[-3:]
    rb = lat_refs[0].shape[0]
    qn = q_ref.shape[0]
    step_heads = range(q_ref.shape[1] // HD)
    weights = [jnp.concatenate([uk_ref[:, lanes(a)], uv_ref[:, lanes(a)]], axis=1) for a in step_heads]
    q = [q_ref[:, lanes(a)] for a in step_heads]
    qq = [jnp.concatenate([x, x], axis=1) for x in q]
    do = [do_ref[:, lanes(a)] for a in step_heads]
    parts = [[] if first == 0 else [triple(refs[pieces].at[a // PAIR], a % PAIR)] for a in step_heads]
    for a in step_heads:
        for i, lat_ref in enumerate(lat_refs):
            rows = pl.ds(i * rb, rb)
            kv = dot(lat_ref[...], weights[a])
            k = kv[:, :HD] * (SCALE * LOG2E)
            hi = k.astype(BF16)
            lo = (k - hi.astype(F32)).astype(BF16)
            k2 = jnp.concatenate([hi, lo], axis=1)
            v = kv[:, HD:].astype(BF16)
            k2_ref[a, rows, :] = k2
            v_ref[a, rows, :] = v
            s = masked(dot(k2, qq[a], NT), gaps_ref[first + i])
            gp = dot(v, do[a], NT)
            m = jnp.maximum(jnp.max(s, axis=0, keepdims=True), -1e30)
            w = jnp.exp2(s - m)
            parts[a].append((m, jnp.sum(w, axis=0, keepdims=True), jnp.sum(w * gp, axis=0, keepdims=True)))
    pad = jnp.zeros((8 - 3 * PAIR, qn), F32)
    for j in range(len(step_heads) // PAIR):
        own = [x for a in range(j * PAIR, (j + 1) * PAIR) for x in join(parts[a])]
        st_ref[j] = jnp.concatenate(own + [pad], axis=0)


def run_stats(first, gaps, pieces, up_key, up_value, queries, grad_out, before):
    rb, depth = pieces[0].shape
    rows = rb * len(pieces)
    heads = queries.shape[1] // HD
    qn = queries.shape[0]
    wide = WIDE * HD
    col = lambda g, *_: (0, g)
    whole = pl.BlockSpec((rb, depth), lambda g, *_: (0, 0))
    st_spec = pl.BlockSpec((WIDE // PAIR, 8, qn), lambda g, *_: (g, 0, 0))
    extra = () if before is None else (before,)
    return pl.pallas_call(
        functools.partial(stats_kernel, first, len(pieces)),
        out_shape=(
            jax.ShapeDtypeStruct((heads, rows, 2 * HD), BF16),
            jax.ShapeDtypeStruct((heads, rows, HD), BF16),
            jax.ShapeDtypeStruct((heads // PAIR, 8, qn), F32),
        ),
        grid_spec=pltpu.PrefetchScalarGridSpec(
            num_scalar_prefetch=1,
            grid=(heads // WIDE,),
            in_specs=[
                pl.BlockSpec((depth, wide), col),
                pl.BlockSpec((depth, wide), col),
                pl.BlockSpec((qn, wide), col),
                pl.BlockSpec((qn, wide), col),
            ]
            + [whole] * len(pieces)
            + [st_spec] * len(extra),
            out_specs=[
                pl.BlockSpec((WIDE, rows, 2 * HD), lambda g, *_: (g, 0, 0)),
                pl.BlockSpec((WIDE, rows, HD), lambda g, *_: (g, 0, 0)),
                st_spec,
            ],
        ),
        compiler_params=pltpu.CompilerParams(vmem_limit_bytes=VMEM),
        cost_estimate=pl.CostEstimate(
            flops=heads * rows * HD * 8 * depth, bytes_accessed=heads * rows * HD * 6, transcendentals=0
        ),
        name="stats",
    )(gaps, up_key, up_value, queries, grad_out, *pieces, *extra)


def head_grads(gaps_ref, q_ref, do_ref, st_refs, blocks, gk_ref, gv_ref):
    qn = q_ref.shape[0]
    pair = range(PAIR)
    q = [q_ref[:, lanes(a)] for a in pair]
    qq = [jnp.concatenate([x, x], axis=1) for x in q]
    do = [do_ref[:, lanes(a)] for a in pair]
    shift, delta = [], []
    for a in pair:
        m, t, d = join([triple(ref, a) for ref in st_refs])
        shift.append(m + jnp.log2(t))
        delta.append(d / t)
    gq = [jnp.zeros((qn, 2 * HD), F32) for a in pair]
    base = 0
    for chunk, k2_ref, v_ref, lower, size in blocks:
        rb = size // 2
        here, rows = pl.ds(lower, size), pl.ds(base, size)
        for a in pair:
            k2 = k2_ref[a, here, :]
            s = dot(k2, qq[a], NT)
            s = jnp.concatenate(
                [masked(s[:rb], gaps_ref[2 * chunk]), masked(s[rb:], gaps_ref[2 * chunk + 1])], axis=0
            )
            gp = dot(v_ref[a, here, :], do[a], NT)
            p = jnp.exp2(s - shift[a])
            ds = (p * (gp - delta[a]) * SCALE).astype(BF16)
            low = p.astype(BF16)
            gk_ref[rows, lanes(a)] = dot(ds, q[a]).astype(BF16)
            gv_ref[rows, lanes(a)] = dot(low, do[a]).astype(BF16)
            gq[a] = gq[a] + dot(ds, k2, TN)
        base += size
    return jnp.concatenate([(x[:, :HD] + x[:, HD:]) * (1.0 / (SCALE * LOG2E)) for x in gq], axis=1)


def up_grads(step, terms, gq, out_ref):
    qn, wide = gq.shape
    n = out_ref.shape[0]
    qb = qn // n
    half = out_ref.shape[2] // 2
    for side in range(2):
        gu = sum(dot(latt, sides[side]) for latt, sides in terms)
        ub = gu.shape[0] // n
        cols = pl.ds(pl.multiple_of(side * half + step * wide, wide), wide)
        for r in range(n):
            lower = r * qb + side * (qb // 2)
            out_ref[r, 0:ub, cols] = gu[r * ub : (r + 1) * ub].astype(BF16)
            out_ref[r, ub:, cols] = gq[lower : lower + qb // 2].astype(BF16)


def whole_kernel(n, held, gaps_ref, q_ref, do_ref, *refs):
    st_refs, refs = refs[:n], refs[n:]
    refs = refs[:5] + refs[5 + held :]
    ka_ref, kb_ref, va_ref, vb_ref, latt_ref, gk_ref, gv_ref, out_ref = refs
    size = ka_ref.shape[1]
    blocks = [(1 + i, kb_ref, vb_ref, i * size, size) for i in range(kb_ref.shape[1] // size)]
    blocks.append((0, ka_ref, va_ref, 0, size))
    gq = head_grads(gaps_ref, q_ref, do_ref, st_refs, blocks, gk_ref, gv_ref)
    terms = [(latt_ref[...], (gk_ref[...], gv_ref[...]))]
    up_grads(pl.program_id(0), terms, gq, out_ref)


def add_latent(gl_ref, own, other):
    total = gl_ref[...]
    for gk, gv, uk, uv in [own, other] if own else [other]:
        total = total + dot(gk[...], uk[...], NT) + dot(gv[...], uv[...], NT)
    gl_ref[...] = total


def put_latent(gl_ref, keep_ref, send_ref):
    steps, rb, _ = keep_ref.shape
    for i in range(steps):
        keep_ref[i] = gl_ref[2 * i * rb : (2 * i + 1) * rb, :].astype(BF16)
        send_ref[i] = gl_ref[(2 * i + 1) * rb : (2 * i + 2) * rb, :].astype(BF16)


def far_kernel(n, chunks, own, gaps_ref, q_ref, do_ref, *refs):
    st_refs, refs = refs[:n], refs[n:]
    k_refs, v_refs, refs = refs[: len(chunks)], refs[len(chunks) : 2 * len(chunks)], refs[2 * len(chunks) :]
    uk_ref, uv_ref, uk2_ref, uv2_ref, ok_ref, ov_ref, gk_ref, gv_ref, gq_ref, keep_ref, send_ref, gl_ref = refs
    step = pl.program_id(0)

    @pl.when(step == 0)
    def _():
        gl_ref[...] = jnp.zeros_like(gl_ref)

    @pl.when(step < own)
    def _():
        blocks = [(c, k, v, 0, k.shape[1]) for c, k, v in zip(chunks, k_refs, v_refs)]
        gq_ref[...] = head_grads(gaps_ref, q_ref, do_ref, st_refs, blocks, gk_ref, gv_ref)
        add_latent(gl_ref, (gk_ref, gv_ref, uk_ref, uv_ref), (ok_ref, ov_ref, uk2_ref, uv2_ref))

    @pl.when(step >= own)
    def _():
        add_latent(gl_ref, None, (ok_ref, ov_ref, uk2_ref, uv2_ref))

    @pl.when(step == pl.num_programs(0) - 1)
    def _():
        put_latent(gl_ref, keep_ref, send_ref)


def near_kernel(n, chunks, own, gaps_ref, q_ref, do_ref, *refs):
    st_refs, refs = refs[:n], refs[n:]
    k_refs, v_refs, refs = refs[: len(chunks)], refs[len(chunks) : 2 * len(chunks)], refs[2 * len(chunks) :]
    uk_ref, uv_ref, uk2_ref, uv2_ref, ok_ref, ov_ref, latt_ref, fk_ref, fv_ref, fq_ref = refs[:10]
    out_ref, keep_ref, send_ref, gk_ref, gv_ref, gl_ref = refs[10:]
    step = pl.program_id(0)

    @pl.when(step == 0)
    def _():
        gl_ref[...] = jnp.zeros_like(gl_ref)

    @pl.when(step < own)
    def _():
        blocks = [(c, k, v, 0, k.shape[1]) for c, k, v in zip(chunks, k_refs, v_refs)]
        gq = fq_ref[...] + head_grads(gaps_ref, q_ref, do_ref, st_refs, blocks, gk_ref, gv_ref)
        rest = fk_ref.shape[0]
        terms = [
            (latt_ref[:, :rest], (fk_ref[...], fv_ref[...])),
            (latt_ref[:, rest:], (gk_ref[...], gv_ref[...])),
        ]
        up_grads(step, terms, gq, out_ref)
        add_latent(gl_ref, (gk_ref, gv_ref, uk_ref, uv_ref), (ok_ref, ov_ref, uk2_ref, uv2_ref))

    @pl.when(step >= own)
    def _():
        add_latent(gl_ref, None, (ok_ref, ov_ref, uk2_ref, uv2_ref))

    @pl.when(step == pl.num_programs(0) - 1)
    def _():
        put_latent(gl_ref, keep_ref, send_ref)


def turn_kernel(*refs):
    rb = refs[0].shape[0]
    for i, ref in enumerate(refs[:-1]):
        refs[-1][:, i * rb : (i + 1) * rb] = ref[...].T


def run_turn(pieces):
    rb, depth = pieces[0].shape
    return pl.pallas_call(
        turn_kernel,
        out_shape=jax.ShapeDtypeStruct((depth, rb * len(pieces)), BF16),
        compiler_params=pltpu.CompilerParams(vmem_limit_bytes=VMEM),
        name="turn",
    )(*pieces)


def part_shape(n, depth, qn, cols):
    return jax.ShapeDtypeStruct((n, depth // n + qn // n // 2, 2 * cols), BF16)


def run_whole(gaps, queries, grad_out, stats, k2, v, latt, lower, upper, pairs, held=()):
    n = len(stats)
    depth = latt.shape[0]
    rows = sum(x.shape[1] for x in k2)
    qn = queries.shape[0]
    wide = PAIR * HD
    cols = (upper - lower) * wide
    col = lambda g, *_: (0, lower + g)
    block = lambda g, *_: (lower + g, 0, 0)
    part = part_shape(n, depth, qn, cols)
    operands = (gaps, queries, grad_out, *stats, *k2, *v, latt)
    return pl.pallas_call(
        functools.partial(whole_kernel, n, len(held)),
        out_shape=(jax.ShapeDtypeStruct((rows, pairs * wide), BF16),) * 2 + (part,),
        grid_spec=pltpu.PrefetchScalarGridSpec(
            num_scalar_prefetch=1,
            grid=(upper - lower,),
            in_specs=[pl.BlockSpec((qn, wide), col)] * 2
            + [pl.BlockSpec((None, 8, qn), block)] * n
            + [pl.BlockSpec((PAIR, *x.shape[1:]), block) for x in (*k2, *v)]
            + [pl.BlockSpec(latt.shape, lambda g, *_: (0, 0))]
            + [pl.BlockSpec(memory_space=pl.ANY)] * len(held),
            out_specs=[pl.BlockSpec((rows, wide), col)] * 2
            + [pl.BlockSpec(part.shape, lambda g, *_: (0, 0, 0))],
        ),
        input_output_aliases={len(operands) + i: i for i in range(len(held))},
        compiler_params=pltpu.CompilerParams(vmem_limit_bytes=VMEM),
        cost_estimate=pl.CostEstimate(
            flops=cols * rows * 2 * (7 * qn + 2 * depth), bytes_accessed=cols * rows * 10, transcendentals=0
        ),
        name="whole",
    )(*operands, *held)


def run_split(far, gaps, queries, grad_out, stats, k2, v, chunks, up_key, up_value, other, first, pairs,
              latt=None, before=()):
    n = len(stats)
    size = k2[0].shape[1]
    depth = up_key.shape[0]
    rb = size // 2
    rows = size * len(chunks)
    qn = queries.shape[0]
    wide = PAIR * HD
    cols = pairs * wide
    last = pairs - 1
    own = lambda g, *_: (0, first + jnp.minimum(g, last))
    own3 = lambda g, *_: (first + jnp.minimum(g, last), 0, 0)
    out = lambda g, *_: (0, jnp.minimum(g, last))
    col = lambda g, *_: (0, g)
    fixed = lambda g, *_: (0, 0)
    fixed3 = lambda g, *_: (0, 0, 0)

    def rows_of(chunk):
        if chunk == 0:
            return 0, own3
        return 1, lambda g, *_: (first + jnp.minimum(g, last), chunk - 1, 0)

    picked = [rows_of(c) for c in chunks]
    in_specs = [pl.BlockSpec((qn, wide), own)] * 2 + [pl.BlockSpec((None, 8, qn), own3)] * n
    in_specs += [pl.BlockSpec((PAIR, size, 2 * HD), index) for _, index in picked]
    in_specs += [pl.BlockSpec((PAIR, size, HD), index) for _, index in picked]
    in_specs += [pl.BlockSpec((depth, wide), own)] * 2 + [pl.BlockSpec((depth, wide), col)] * 2
    in_specs += [pl.BlockSpec((rows, wide), lambda g, *_: (0 if far else other[0].shape[0] // rows - 1, g))] * 2
    grads = (jax.ShapeDtypeStruct((rows, cols), BF16),) * 2
    sums = (jax.ShapeDtypeStruct((len(chunks), rb, depth), BF16),) * 2
    sum_specs = [pl.BlockSpec(sums[0].shape, fixed3)] * 2
    gl = pltpu.VMEM((rows, depth), F32)
    if far:
        kernel = far_kernel
        out_shape = grads + (jax.ShapeDtypeStruct((qn, cols), F32),) + sums
        out_specs = [pl.BlockSpec((rows, wide), out)] * 2 + [pl.BlockSpec((qn, wide), out)] + sum_specs
        scratch = [gl]
    else:
        kernel = near_kernel
        part = part_shape(n, depth, qn, cols)
        in_specs += [pl.BlockSpec(latt.shape, fixed)]
        in_specs += [pl.BlockSpec((before[0].shape[0], wide), out)] * 2 + [pl.BlockSpec((qn, wide), out)]
        out_shape = (part,) + sums
        out_specs = [pl.BlockSpec(part.shape, fixed3)] + sum_specs
        scratch = [pltpu.VMEM((rows, wide), BF16)] * 2
        scratch += [gl]
    return pl.pallas_call(
        functools.partial(kernel, n, chunks, pairs),
        out_shape=out_shape,
        grid_spec=pltpu.PrefetchScalarGridSpec(
            num_scalar_prefetch=1,
            grid=(first,),
            in_specs=in_specs,
            out_specs=out_specs,
            scratch_shapes=scratch,
        ),
        compiler_params=pltpu.CompilerParams(vmem_limit_bytes=VMEM),
        cost_estimate=pl.CostEstimate(
            flops=cols * rows * 2 * (7 * qn + 4 * depth) + first * wide * rows * 4 * depth,
            bytes_accessed=cols * rows * 10,
            transcendentals=0,
        ),
        name="far" if far else "near",
    )(gaps, queries, grad_out, *stats, *[k2[i] for i, _ in picked], *[v[i] for i, _ in picked],
      up_key, up_value, up_key, up_value, *other, *([] if far else [latt]), *before)


def after(value, *others):
    return lax.optimization_barrier((value, *others))[0]


def local(queries, grad_out, latent, up_key, up_value):
    heads = queries.shape[1] // HD
    qn = queries.shape[0]
    n = lax.axis_size("ctx")
    mates = lax.axis_size("head")
    rb, depth = latent.shape
    chunks = mates // 2
    near = 1

    firsts = [latent] + [swap(latent, "head", 2 * k) for k in range(1, chunks)]
    starts = (lax.axis_index("ctx") * mates + (lax.axis_index("head") ^ jnp.arange(mates))) * rb
    gaps = (rb * mates * n - qn - starts).astype(jnp.int32)
    k2, v, every, stats = [], [], [], None
    for which in ([0], list(range(1, chunks))):
        pieces = []
        for c in which:
            mine = firsts[c] if stats is None else after(firsts[c], stats)
            pieces += [mine, swap(mine, "head", 1)]
        one_k2, one_v, stats = run_stats(
            2 * which[0], gaps, pieces, up_key, up_value, queries, grad_out, stats
        )
        k2.append(one_k2)
        v.append(one_v)
        every += pieces
    latt = run_turn([after(every[2], stats)] + every[3:] + every[:2])
    stats = [stats] + [swap(stats, "ctx", k) for k in range(1, n)]

    pairs = heads // PAIR
    first = 3 * pairs // 4
    half = first // 3
    held, outs = (), []
    for lower, upper in ((0, half), (half, first)):
        gk, gv, part = run_whole(gaps, queries, grad_out, stats, k2, v, latt, lower, upper, first, held)
        held = (gk, gv)
        outs.append(lax.all_to_all(part, "ctx", 0, 0, tiled=True))
    split = functools.partial(run_split, up_key=up_key, up_value=up_value, other=(gk, gv), first=first,
                              pairs=pairs - first, queries=queries, grad_out=grad_out, stats=stats, k2=k2, v=v)
    fk, fv, fq, far, far_away = split(True, after(gaps, outs[0]), chunks=list(range(near, chunks)))
    far = far.astype(F32) + swap(far_away, "head", 1).astype(F32)
    far = far.astype(BF16)
    part, close, close_away = split(
        False, after(gaps, far), chunks=list(range(near)), latt=latt, before=(fk, fv, fq)
    )
    outs.append(lax.all_to_all(after(part, outs[1]), "ctx", 0, 0, tiled=True))
    got = [swap(far[k], "head", 2 * (near + k)) for k in range(chunks - near)]
    close = close.astype(F32) + swap(after(close_away, *got), "head", 1).astype(F32)
    grad_latent = close[0]
    for x in got:
        grad_latent = grad_latent + x.astype(F32)

    sums = [jnp.sum(o.astype(F32), axis=0) for o in outs]
    ub = depth // n
    grad_key = jnp.concatenate([s[:ub, : s.shape[1] // 2] for s in sums], axis=1)
    grad_value = jnp.concatenate([s[:ub, s.shape[1] // 2 :] for s in sums], axis=1)
    grad_q = jnp.concatenate(
        [jnp.concatenate([s[ub:, : s.shape[1] // 2], s[ub:, s.shape[1] // 2 :]], axis=0) for s in sums], axis=1
    )
    return (grad_q, grad_latent, grad_key, grad_value)


def solution(mesh):
    return jax.shard_map(
        local,
        mesh=mesh,
        in_specs=(
            P(None, "head"),
            P(None, "head"),
            P(("ctx", "head"), None),
            P(None, "head"),
            P(None, "head"),
        ),
        out_specs=(P("ctx", "head"), P(("ctx", "head"), None), P("ctx", "head"), P("ctx", "head")),
        check_vma=False,
    )
```

```python
import functools
import math

import jax
import jax.numpy as jnp
from jax import lax
from jax.experimental import pallas as pl
from jax.experimental.pallas import tpu as pltpu
from jax.sharding import PartitionSpec as P

HD = 128
PAIR = 2
WIDE = 4
VMEM = 60 << 20
NT = (((1,), (1,)), ((), ()))
TN = (((0,), (0,)), ((), ()))
NN = (((1,), (0,)), ((), ()))
SCALE = 1.0 / math.sqrt(HD)
LOG2E = math.log2(math.e)
F32 = jnp.float32
BF16 = jnp.bfloat16


def dot(a, b, dims=NN):
    return lax.dot_general(a, b, dims, preferred_element_type=F32)


def swap(array, axis, distance):
    count = lax.axis_size(axis)
    return lax.ppermute(array, axis, [(i, i ^ distance) for i in range(count)])


def masked(s, gap):
    rows = lax.broadcasted_iota(jnp.int32, s.shape, 0)
    cols = lax.broadcasted_iota(jnp.int32, s.shape, 1)
    return jnp.where(rows - cols > gap, -jnp.inf, s)


def lanes(head):
    return slice(head * HD, (head + 1) * HD)


def join(parts):
    m = functools.reduce(jnp.maximum, [p[0] for p in parts])
    factors = [jnp.exp2(p[0] - m) for p in parts]
    t = sum(p[1] * f for p, f in zip(parts, factors))
    d = sum(p[2] * f for p, f in zip(parts, factors))
    return m, t, d


def triple(ref, head):
    return tuple(ref[3 * head + i : 3 * head + i + 1, :] for i in range(3))


def stats_kernel(first, pieces, gaps_ref, uk_ref, uv_ref, q_ref, do_ref, *refs):
    lat_refs = refs[:pieces]
    k2_ref, v_ref, st_ref = refs[-3:]
    rb = lat_refs[0].shape[0]
    qn = q_ref.shape[0]
    step_heads = range(q_ref.shape[1] // HD)
    weights = [jnp.concatenate([uk_ref[:, lanes(a)], uv_ref[:, lanes(a)]], axis=1) for a in step_heads]
    q = [q_ref[:, lanes(a)] for a in step_heads]
    qq = [jnp.concatenate([x, x], axis=1) for x in q]
    do = [do_ref[:, lanes(a)] for a in step_heads]
    parts = [[] if first == 0 else [triple(refs[pieces].at[a // PAIR], a % PAIR)] for a in step_heads]
    for a in step_heads:
        for i, lat_ref in enumerate(lat_refs):
            rows = pl.ds(i * rb, rb)
            kv = dot(lat_ref[...], weights[a])
            k = kv[:, :HD] * (SCALE * LOG2E)
            hi = k.astype(BF16)
            lo = (k - hi.astype(F32)).astype(BF16)
            k2 = jnp.concatenate([hi, lo], axis=1)
            v = kv[:, HD:].astype(BF16)
            k2_ref[a, rows, :] = k2
            v_ref[a, rows, :] = v
            s = masked(dot(k2, qq[a], NT), gaps_ref[first + i])
            gp = dot(v, do[a], NT)
            m = jnp.maximum(jnp.max(s, axis=0, keepdims=True), -1e30)
            w = jnp.exp2(s - m)
            parts[a].append((m, jnp.sum(w, axis=0, keepdims=True), jnp.sum(w * gp, axis=0, keepdims=True)))
    pad = jnp.zeros((8 - 3 * PAIR, qn), F32)
    for j in range(len(step_heads) // PAIR):
        own = [x for a in range(j * PAIR, (j + 1) * PAIR) for x in join(parts[a])]
        st_ref[j] = jnp.concatenate(own + [pad], axis=0)


def run_stats(first, gaps, pieces, up_key, up_value, queries, grad_out, before):
    rb, depth = pieces[0].shape
    rows = rb * len(pieces)
    heads = queries.shape[1] // HD
    qn = queries.shape[0]
    wide = WIDE * HD
    col = lambda g, *_: (0, g)
    whole = pl.BlockSpec((rb, depth), lambda g, *_: (0, 0))
    st_spec = pl.BlockSpec((WIDE // PAIR, 8, qn), lambda g, *_: (g, 0, 0))
    extra = () if before is None else (before,)
    return pl.pallas_call(
        functools.partial(stats_kernel, first, len(pieces)),
        out_shape=(
            jax.ShapeDtypeStruct((heads, rows, 2 * HD), BF16),
            jax.ShapeDtypeStruct((heads, rows, HD), BF16),
            jax.ShapeDtypeStruct((heads // PAIR, 8, qn), F32),
        ),
        grid_spec=pltpu.PrefetchScalarGridSpec(
            num_scalar_prefetch=1,
            grid=(heads // WIDE,),
            in_specs=[
                pl.BlockSpec((depth, wide), col),
                pl.BlockSpec((depth, wide), col),
                pl.BlockSpec((qn, wide), col),
                pl.BlockSpec((qn, wide), col),
            ]
            + [whole] * len(pieces)
            + [st_spec] * len(extra),
            out_specs=[
                pl.BlockSpec((WIDE, rows, 2 * HD), lambda g, *_: (g, 0, 0)),
                pl.BlockSpec((WIDE, rows, HD), lambda g, *_: (g, 0, 0)),
                st_spec,
            ],
        ),
        compiler_params=pltpu.CompilerParams(vmem_limit_bytes=VMEM),
        cost_estimate=pl.CostEstimate(
            flops=heads * rows * HD * 8 * depth, bytes_accessed=heads * rows * HD * 6, transcendentals=0
        ),
        name="stats",
    )(gaps, up_key, up_value, queries, grad_out, *pieces, *extra)


def head_grads(gaps_ref, q_ref, do_ref, st_refs, blocks, gk_ref, gv_ref):
    qn = q_ref.shape[0]
    pair = range(PAIR)
    q = [q_ref[:, lanes(a)] for a in pair]
    qq = [jnp.concatenate([x, x], axis=1) for x in q]
    do = [do_ref[:, lanes(a)] for a in pair]
    shift, delta = [], []
    for a in pair:
        m, t, d = join([triple(ref, a) for ref in st_refs])
        shift.append(m + jnp.log2(t))
        delta.append(d / t)
    gq = [jnp.zeros((qn, 2 * HD), F32) for a in pair]
    base = 0
    for chunk, k2_ref, v_ref, lower, size in blocks:
        rb = size // 2
        here, rows = pl.ds(lower, size), pl.ds(base, size)
        for a in pair:
            k2 = k2_ref[a, here, :]
            s = dot(k2, qq[a], NT)
            s = jnp.concatenate(
                [masked(s[:rb], gaps_ref[2 * chunk]), masked(s[rb:], gaps_ref[2 * chunk + 1])], axis=0
            )
            gp = dot(v_ref[a, here, :], do[a], NT)
            p = jnp.exp2(s - shift[a])
            ds = (p * (gp - delta[a]) * SCALE).astype(BF16)
            low = p.astype(BF16)
            gk_ref[rows, lanes(a)] = dot(ds, q[a]).astype(BF16)
            gv_ref[rows, lanes(a)] = dot(low, do[a]).astype(BF16)
            gq[a] = gq[a] + dot(ds, k2, TN)
        base += size
    return jnp.concatenate([(x[:, :HD] + x[:, HD:]) * (1.0 / (SCALE * LOG2E)) for x in gq], axis=1)


def up_grads(step, terms, gq, out_ref):
    qn, wide = gq.shape
    n = out_ref.shape[0]
    qb = qn // n
    half = out_ref.shape[2] // 2
    for side in range(2):
        gu = sum(dot(latt, sides[side]) for latt, sides in terms)
        ub = gu.shape[0] // n
        cols = pl.ds(pl.multiple_of(side * half + step * wide, wide), wide)
        for r in range(n):
            lower = r * qb + side * (qb // 2)
            out_ref[r, 0:ub, cols] = gu[r * ub : (r + 1) * ub].astype(BF16)
            out_ref[r, ub:, cols] = gq[lower : lower + qb // 2].astype(BF16)


def whole_kernel(n, held, gaps_ref, q_ref, do_ref, *refs):
    st_refs, refs = refs[:n], refs[n:]
    refs = refs[:5] + refs[5 + held :]
    ka_ref, kb_ref, va_ref, vb_ref, latt_ref, gk_ref, gv_ref, out_ref = refs
    size = ka_ref.shape[1]
    blocks = [(1 + i, kb_ref, vb_ref, i * size, size) for i in range(kb_ref.shape[1] // size)]
    blocks.append((0, ka_ref, va_ref, 0, size))
    gq = head_grads(gaps_ref, q_ref, do_ref, st_refs, blocks, gk_ref, gv_ref)
    terms = [(latt_ref[...], (gk_ref[...], gv_ref[...]))]
    up_grads(pl.program_id(0), terms, gq, out_ref)


def add_latent(gl_ref, own, other, keep_ref, send_ref):
    step = pl.program_id(0)
    steps, rb, _ = keep_ref.shape
    for i in range(2 * steps):
        rows = pl.ds(i * rb, rb)
        total = jnp.where(step == 0, 0.0, gl_ref[rows, :])
        for gk, gv, uk, uv in (own, other):
            total = total + dot(gk[rows, :], uk[...], NT) + dot(gv[rows, :], uv[...], NT)
        gl_ref[rows, :] = total
        out_ref = send_ref if i % 2 else keep_ref
        out_ref[i // 2] = total.astype(BF16)


def far_kernel(n, chunks, gaps_ref, q_ref, do_ref, *refs):
    st_refs, refs = refs[:n], refs[n:]
    k_refs, v_refs, refs = refs[: len(chunks)], refs[len(chunks) : 2 * len(chunks)], refs[2 * len(chunks) :]
    uk_ref, uv_ref, uk2_ref, uv2_ref, ok_ref, ov_ref, gk_ref, gv_ref, gq_ref, keep_ref, send_ref, gl_ref = refs
    blocks = [(c, k, v, 0, k.shape[1]) for c, k, v in zip(chunks, k_refs, v_refs)]
    gq_ref[...] = head_grads(gaps_ref, q_ref, do_ref, st_refs, blocks, gk_ref, gv_ref)
    add_latent(gl_ref, (gk_ref, gv_ref, uk_ref, uv_ref), (ok_ref, ov_ref, uk2_ref, uv2_ref), keep_ref, send_ref)


def near_kernel(n, chunks, gaps_ref, q_ref, do_ref, *refs):
    st_refs, refs = refs[:n], refs[n:]
    k_refs, v_refs, refs = refs[: len(chunks)], refs[len(chunks) : 2 * len(chunks)], refs[2 * len(chunks) :]
    uk_ref, uv_ref, uk2_ref, uv2_ref, ok_ref, ov_ref, latt_ref, fk_ref, fv_ref, fq_ref = refs[:10]
    out_ref, keep_ref, send_ref, gk_ref, gv_ref, gl_ref = refs[10:]
    blocks = [(c, k, v, 0, k.shape[1]) for c, k, v in zip(chunks, k_refs, v_refs)]
    gq = fq_ref[...] + head_grads(gaps_ref, q_ref, do_ref, st_refs, blocks, gk_ref, gv_ref)
    rest = fk_ref.shape[0]
    terms = [
        (latt_ref[:, :rest], (fk_ref[...], fv_ref[...])),
        (latt_ref[:, rest:], (gk_ref[...], gv_ref[...])),
    ]
    up_grads(pl.program_id(0), terms, gq, out_ref)
    add_latent(gl_ref, (gk_ref, gv_ref, uk_ref, uv_ref), (ok_ref, ov_ref, uk2_ref, uv2_ref), keep_ref, send_ref)


def turn_kernel(*refs):
    rb = refs[0].shape[0]
    for i, ref in enumerate(refs[:-1]):
        refs[-1][:, i * rb : (i + 1) * rb] = ref[...].T


def run_turn(pieces):
    rb, depth = pieces[0].shape
    return pl.pallas_call(
        turn_kernel,
        out_shape=jax.ShapeDtypeStruct((depth, rb * len(pieces)), BF16),
        compiler_params=pltpu.CompilerParams(vmem_limit_bytes=VMEM),
        name="turn",
    )(*pieces)


def part_shape(n, depth, qn, cols):
    return jax.ShapeDtypeStruct((n, depth // n + qn // n // 2, 2 * cols), BF16)


def run_whole(gaps, queries, grad_out, stats, k2, v, latt, lower, upper, pairs, held=()):
    n = len(stats)
    depth = latt.shape[0]
    rows = sum(x.shape[1] for x in k2)
    qn = queries.shape[0]
    wide = PAIR * HD
    cols = (upper - lower) * wide
    col = lambda g, *_: (0, lower + g)
    block = lambda g, *_: (lower + g, 0, 0)
    part = part_shape(n, depth, qn, cols)
    operands = (gaps, queries, grad_out, *stats, *k2, *v, latt)
    return pl.pallas_call(
        functools.partial(whole_kernel, n, len(held)),
        out_shape=(jax.ShapeDtypeStruct((rows, pairs * wide), BF16),) * 2 + (part,),
        grid_spec=pltpu.PrefetchScalarGridSpec(
            num_scalar_prefetch=1,
            grid=(upper - lower,),
            in_specs=[pl.BlockSpec((qn, wide), col)] * 2
            + [pl.BlockSpec((None, 8, qn), block)] * n
            + [pl.BlockSpec((PAIR, *x.shape[1:]), block) for x in (*k2, *v)]
            + [pl.BlockSpec(latt.shape, lambda g, *_: (0, 0))]
            + [pl.BlockSpec(memory_space=pl.ANY)] * len(held),
            out_specs=[pl.BlockSpec((rows, wide), col)] * 2
            + [pl.BlockSpec(part.shape, lambda g, *_: (0, 0, 0))],
        ),
        input_output_aliases={len(operands) + i: i for i in range(len(held))},
        compiler_params=pltpu.CompilerParams(vmem_limit_bytes=VMEM),
        cost_estimate=pl.CostEstimate(
            flops=cols * rows * 2 * (7 * qn + 2 * depth), bytes_accessed=cols * rows * 10, transcendentals=0
        ),
        name="whole",
    )(*operands, *held)


def run_split(far, gaps, queries, grad_out, stats, k2, v, chunks, up_key, up_value, other, first, pairs,
              latt=None, before=()):
    n = len(stats)
    size = k2[0].shape[1]
    depth = up_key.shape[0]
    rb = size // 2
    rows = size * len(chunks)
    qn = queries.shape[0]
    wide = PAIR * HD
    cols = pairs * wide
    span = first // pairs * wide
    own = lambda g, *_: (0, first + g)
    own3 = lambda g, *_: (first + g, 0, 0)
    out = col = lambda g, *_: (0, g)
    fixed = lambda g, *_: (0, 0)
    fixed3 = lambda g, *_: (0, 0, 0)

    def rows_of(chunk):
        if chunk == 0:
            return 0, own3
        return 1, lambda g, *_: (first + g, chunk - 1, 0)

    picked = [rows_of(c) for c in chunks]
    in_specs = [pl.BlockSpec((qn, wide), own)] * 2 + [pl.BlockSpec((None, 8, qn), own3)] * n
    in_specs += [pl.BlockSpec((PAIR, size, 2 * HD), index) for _, index in picked]
    in_specs += [pl.BlockSpec((PAIR, size, HD), index) for _, index in picked]
    in_specs += [pl.BlockSpec((depth, wide), own)] * 2 + [pl.BlockSpec((depth, span), col)] * 2
    in_specs += [pl.BlockSpec((rows, span), lambda g, *_: (0 if far else other[0].shape[0] // rows - 1, g))] * 2
    grads = (jax.ShapeDtypeStruct((rows, cols), BF16),) * 2
    sums = (jax.ShapeDtypeStruct((len(chunks), rb, depth), BF16),) * 2
    sum_specs = [pl.BlockSpec(sums[0].shape, fixed3)] * 2
    gl = pltpu.VMEM((rows, depth), F32)
    if far:
        kernel = far_kernel
        out_shape = grads + (jax.ShapeDtypeStruct((qn, cols), F32),) + sums
        out_specs = [pl.BlockSpec((rows, wide), out)] * 2 + [pl.BlockSpec((qn, wide), out)] + sum_specs
        scratch = [gl]
    else:
        kernel = near_kernel
        part = part_shape(n, depth, qn, cols)
        in_specs += [pl.BlockSpec(latt.shape, fixed)]
        in_specs += [pl.BlockSpec((before[0].shape[0], wide), out)] * 2 + [pl.BlockSpec((qn, wide), out)]
        out_shape = (part,) + sums
        out_specs = [pl.BlockSpec(part.shape, fixed3)] + sum_specs
        scratch = [pltpu.VMEM((rows, wide), BF16)] * 2
        scratch += [gl]
    return pl.pallas_call(
        functools.partial(kernel, n, chunks),
        out_shape=out_shape,
        grid_spec=pltpu.PrefetchScalarGridSpec(
            num_scalar_prefetch=1,
            grid=(pairs,),
            in_specs=in_specs,
            out_specs=out_specs,
            scratch_shapes=scratch,
        ),
        compiler_params=pltpu.CompilerParams(vmem_limit_bytes=VMEM),
        cost_estimate=pl.CostEstimate(
            flops=cols * rows * 2 * (7 * qn + 4 * depth) + first * wide * rows * 4 * depth,
            bytes_accessed=cols * rows * 10,
            transcendentals=0,
        ),
        name="far" if far else "near",
    )(gaps, queries, grad_out, *stats, *[k2[i] for i, _ in picked], *[v[i] for i, _ in picked],
      up_key, up_value, up_key, up_value, *other, *([] if far else [latt]), *before)


def after(value, *others):
    return lax.optimization_barrier((value, *others))[0]


def local(queries, grad_out, latent, up_key, up_value):
    heads = queries.shape[1] // HD
    qn = queries.shape[0]
    n = lax.axis_size("ctx")
    mates = lax.axis_size("head")
    rb, depth = latent.shape
    chunks = mates // 2
    near = 1

    firsts = [latent] + [swap(latent, "head", 2 * k) for k in range(1, chunks)]
    starts = (lax.axis_index("ctx") * mates + (lax.axis_index("head") ^ jnp.arange(mates))) * rb
    gaps = (rb * mates * n - qn - starts).astype(jnp.int32)
    k2, v, every, stats = [], [], [], None
    for which in ([0], list(range(1, chunks))):
        pieces = []
        for c in which:
            mine = firsts[c] if stats is None else after(firsts[c], stats)
            pieces += [mine, swap(mine, "head", 1)]
        one_k2, one_v, stats = run_stats(
            2 * which[0], gaps, pieces, up_key, up_value, queries, grad_out, stats
        )
        k2.append(one_k2)
        v.append(one_v)
        every += pieces
    latt = run_turn([after(every[2], stats)] + every[3:] + every[:2])
    stats = [stats] + [swap(stats, "ctx", k) for k in range(1, n)]

    pairs = heads // PAIR
    first = 3 * pairs // 4
    held, outs = (), []
    for lower, upper in ((0, first),):
        gk, gv, part = run_whole(gaps, queries, grad_out, stats, k2, v, latt, lower, upper, first, held)
        held = (gk, gv)
        outs.append(lax.all_to_all(part, "ctx", 0, 0, tiled=True))
    split = functools.partial(run_split, up_key=up_key, up_value=up_value, other=(gk, gv), first=first,
                              pairs=pairs - first, queries=queries, grad_out=grad_out, stats=stats, k2=k2, v=v)
    fk, fv, fq, far, far_away = split(True, gaps, chunks=list(range(near, chunks)))
    far = far.astype(F32) + swap(far_away, "head", 1).astype(F32)
    far = far.astype(BF16)
    part, close, close_away = split(
        False, after(gaps, far), chunks=list(range(near)), latt=latt, before=(fk, fv, fq)
    )
    outs.append(lax.all_to_all(after(part, outs[0]), "ctx", 0, 0, tiled=True))
    got = [swap(far[k], "head", 2 * (near + k)) for k in range(chunks - near)]
    close = close.astype(F32) + swap(after(close_away, outs[1], *got), "head", 1).astype(F32)
    grad_latent = close[0]
    for x in got:
        grad_latent = grad_latent + x.astype(F32)

    sums = [functools.reduce(jnp.add, [o[k].astype(F32) for k in range(n)]) for o in outs]
    ub = depth // n
    grad_key = jnp.concatenate([s[:ub, : s.shape[1] // 2] for s in sums], axis=1)
    grad_value = jnp.concatenate([s[:ub, s.shape[1] // 2 :] for s in sums], axis=1)
    grad_q = jnp.concatenate(
        [jnp.concatenate([s[ub:, : s.shape[1] // 2], s[ub:, s.shape[1] // 2 :]], axis=0) for s in sums], axis=1
    )
    return (grad_q, grad_latent, grad_key, grad_value)


def solution(mesh):
    return jax.shard_map(
        local,
        mesh=mesh,
        in_specs=(
            P(None, "head"),
            P(None, "head"),
            P(("ctx", "head"), None),
            P(None, "head"),
            P(None, "head"),
        ),
        out_specs=(P("ctx", "head"), P(("ctx", "head"), None), P("ctx", "head"), P("ctx", "head")),
        check_vma=False,
    )
```

```python
import functools
import math

import jax
import jax.numpy as jnp
from jax import lax
from jax.experimental import pallas as pl
from jax.experimental.pallas import tpu as pltpu
from jax.sharding import PartitionSpec as P

HD = 128
PAIR = 2
WIDE = 4
VMEM = 60 << 20
NT = (((1,), (1,)), ((), ()))
TN = (((0,), (0,)), ((), ()))
NN = (((1,), (0,)), ((), ()))
SCALE = 1.0 / math.sqrt(HD)
LOG2E = math.log2(math.e)
F32 = jnp.float32
BF16 = jnp.bfloat16


def dot(a, b, dims=NN):
    return lax.dot_general(a, b, dims, preferred_element_type=F32)


def swap(array, axis, distance):
    count = lax.axis_size(axis)
    return lax.ppermute(array, axis, [(i, i ^ distance) for i in range(count)])


def masked(s, gap):
    rows = lax.broadcasted_iota(jnp.int32, s.shape, 0)
    cols = lax.broadcasted_iota(jnp.int32, s.shape, 1)
    return jnp.where(rows - cols > gap, -jnp.inf, s)


def lanes(head):
    return slice(head * HD, (head + 1) * HD)


def join(parts):
    m = functools.reduce(jnp.maximum, [p[0] for p in parts])
    factors = [jnp.exp2(p[0] - m) for p in parts]
    t = sum(p[1] * f for p, f in zip(parts, factors))
    d = sum(p[2] * f for p, f in zip(parts, factors))
    return m, t, d


def triple(ref, head):
    return tuple(ref[3 * head + i : 3 * head + i + 1, :] for i in range(3))


def stats_kernel(first, pieces, gaps_ref, uk_ref, uv_ref, q_ref, do_ref, *refs):
    lat_refs = refs[:pieces]
    k2_ref, gp_ref, st_ref = refs[-3:]
    rb = lat_refs[0].shape[0]
    qn = q_ref.shape[0]
    step_heads = range(q_ref.shape[1] // HD)
    weights = [jnp.concatenate([uk_ref[:, lanes(a)], uv_ref[:, lanes(a)]], axis=1) for a in step_heads]
    q = [q_ref[:, lanes(a)] for a in step_heads]
    qq = [jnp.concatenate([x, x], axis=1) for x in q]
    do = [do_ref[:, lanes(a)] for a in step_heads]
    parts = [[] if first == 0 else [triple(refs[pieces].at[a // PAIR], a % PAIR)] for a in step_heads]
    for a in step_heads:
        for i, lat_ref in enumerate(lat_refs):
            rows = pl.ds(i * rb, rb)
            kv = dot(lat_ref[...], weights[a])
            k = kv[:, :HD] * (SCALE * LOG2E)
            hi = k.astype(BF16)
            lo = (k - hi.astype(F32)).astype(BF16)
            k2 = jnp.concatenate([hi, lo], axis=1)
            v = kv[:, HD:].astype(BF16)
            k2_ref[a, rows, :] = k2
            s = masked(dot(k2, qq[a], NT), gaps_ref[first + i])
            gp = dot(v, do[a], NT)
            gp_ref[a, rows, :] = gp
            m = jnp.maximum(jnp.max(s, axis=0, keepdims=True), -1e30)
            w = jnp.exp2(s - m)
            parts[a].append((m, jnp.sum(w, axis=0, keepdims=True), jnp.sum(w * gp, axis=0, keepdims=True)))
    pad = jnp.zeros((8 - 3 * PAIR, qn), F32)
    for j in range(len(step_heads) // PAIR):
        own = [x for a in range(j * PAIR, (j + 1) * PAIR) for x in join(parts[a])]
        st_ref[j] = jnp.concatenate(own + [pad], axis=0)


def run_stats(first, gaps, pieces, up_key, up_value, queries, grad_out, before):
    rb, depth = pieces[0].shape
    rows = rb * len(pieces)
    heads = queries.shape[1] // HD
    qn = queries.shape[0]
    wide = WIDE * HD
    col = lambda g, *_: (0, g)
    whole = pl.BlockSpec((rb, depth), lambda g, *_: (0, 0))
    st_spec = pl.BlockSpec((WIDE // PAIR, 8, qn), lambda g, *_: (g, 0, 0))
    extra = () if before is None else (before,)
    return pl.pallas_call(
        functools.partial(stats_kernel, first, len(pieces)),
        out_shape=(
            jax.ShapeDtypeStruct((heads, rows, 2 * HD), BF16),
            jax.ShapeDtypeStruct((heads, rows, qn), F32),
            jax.ShapeDtypeStruct((heads // PAIR, 8, qn), F32),
        ),
        grid_spec=pltpu.PrefetchScalarGridSpec(
            num_scalar_prefetch=1,
            grid=(heads // WIDE,),
            in_specs=[
                pl.BlockSpec((depth, wide), col),
                pl.BlockSpec((depth, wide), col),
                pl.BlockSpec((qn, wide), col),
                pl.BlockSpec((qn, wide), col),
            ]
            + [whole] * len(pieces)
            + [st_spec] * len(extra),
            out_specs=[
                pl.BlockSpec((WIDE, rows, 2 * HD), lambda g, *_: (g, 0, 0)),
                pl.BlockSpec((WIDE, rows, qn), lambda g, *_: (g, 0, 0)),
                st_spec,
            ],
        ),
        compiler_params=pltpu.CompilerParams(vmem_limit_bytes=VMEM),
        cost_estimate=pl.CostEstimate(
            flops=heads * rows * HD * 8 * depth, bytes_accessed=heads * rows * HD * 6, transcendentals=0
        ),
        name="stats",
    )(gaps, up_key, up_value, queries, grad_out, *pieces, *extra)


def head_grads(gaps_ref, q_ref, do_ref, st_refs, blocks, gk_ref, gv_ref):
    qn = q_ref.shape[0]
    pair = range(PAIR)
    q = [q_ref[:, lanes(a)] for a in pair]
    qq = [jnp.concatenate([x, x], axis=1) for x in q]
    do = [do_ref[:, lanes(a)] for a in pair]
    shift, delta = [], []
    for a in pair:
        m, t, d = join([triple(ref, a) for ref in st_refs])
        shift.append(m + jnp.log2(t))
        delta.append(d / t)
    gq = [jnp.zeros((qn, 2 * HD), F32) for a in pair]
    base = 0
    for chunk, k2_ref, gp_ref, lower, size in blocks:
        rb = size // 2
        here, rows = pl.ds(lower, size), pl.ds(base, size)
        for a in pair:
            k2 = k2_ref[a, here, :]
            s = dot(k2, qq[a], NT)
            s = jnp.concatenate(
                [masked(s[:rb], gaps_ref[2 * chunk]), masked(s[rb:], gaps_ref[2 * chunk + 1])], axis=0
            )
            gp = gp_ref[a, here, :]
            p = jnp.exp2(s - shift[a])
            ds = (p * (gp - delta[a]) * SCALE).astype(BF16)
            low = p.astype(BF16)
            gk_ref[rows, lanes(a)] = dot(ds, q[a]).astype(BF16)
            gv_ref[rows, lanes(a)] = dot(low, do[a]).astype(BF16)
            gq[a] = gq[a] + dot(ds, k2, TN)
        base += size
    return jnp.concatenate([(x[:, :HD] + x[:, HD:]) * (1.0 / (SCALE * LOG2E)) for x in gq], axis=1)


def up_grads(step, terms, gq, out_ref):
    qn, wide = gq.shape
    n = out_ref.shape[0]
    qb = qn // n
    half = out_ref.shape[2] // 2
    for side in range(2):
        gu = sum(dot(latt, sides[side]) for latt, sides in terms)
        ub = gu.shape[0] // n
        cols = pl.ds(pl.multiple_of(side * half + step * wide, wide), wide)
        for r in range(n):
            lower = r * qb + side * (qb // 2)
            out_ref[r, 0:ub, cols] = gu[r * ub : (r + 1) * ub].astype(BF16)
            out_ref[r, ub:, cols] = gq[lower : lower + qb // 2].astype(BF16)


def whole_kernel(n, held, gaps_ref, q_ref, do_ref, *refs):
    st_refs, refs = refs[:n], refs[n:]
    refs = refs[:5] + refs[5 + held :]
    ka_ref, kb_ref, va_ref, vb_ref, latt_ref, gk_ref, gv_ref, out_ref = refs
    size = ka_ref.shape[1]
    blocks = [(1 + i, kb_ref, vb_ref, i * size, size) for i in range(kb_ref.shape[1] // size)]
    blocks.append((0, ka_ref, va_ref, 0, size))
    gq = head_grads(gaps_ref, q_ref, do_ref, st_refs, blocks, gk_ref, gv_ref)
    terms = [(latt_ref[...], (gk_ref[...], gv_ref[...]))]
    up_grads(pl.program_id(0), terms, gq, out_ref)


def add_latent(gl_ref, own, other, keep_ref, send_ref):
    step = pl.program_id(0)
    steps, rb, _ = keep_ref.shape
    for i in range(2 * steps):
        rows = pl.ds(i * rb, rb)
        total = jnp.where(step == 0, 0.0, gl_ref[rows, :])
        for gk, gv, uk, uv in (own, other):
            total = total + dot(gk[rows, :], uk[...], NT) + dot(gv[rows, :], uv[...], NT)
        gl_ref[rows, :] = total
        out_ref = send_ref if i % 2 else keep_ref
        out_ref[i // 2] = total.astype(BF16)


def far_kernel(n, chunks, gaps_ref, q_ref, do_ref, *refs):
    st_refs, refs = refs[:n], refs[n:]
    k_refs, gp_refs, refs = refs[: len(chunks)], refs[len(chunks) : 2 * len(chunks)], refs[2 * len(chunks) :]
    uk_ref, uv_ref, uk2_ref, uv2_ref, ok_ref, ov_ref, gk_ref, gv_ref, gq_ref, keep_ref, send_ref, gl_ref = refs
    blocks = [(c, k, v, 0, k.shape[1]) for c, k, v in zip(chunks, k_refs, gp_refs)]
    gq_ref[...] = head_grads(gaps_ref, q_ref, do_ref, st_refs, blocks, gk_ref, gv_ref)
    add_latent(gl_ref, (gk_ref, gv_ref, uk_ref, uv_ref), (ok_ref, ov_ref, uk2_ref, uv2_ref), keep_ref, send_ref)


def near_kernel(n, chunks, gaps_ref, q_ref, do_ref, *refs):
    st_refs, refs = refs[:n], refs[n:]
    k_refs, gp_refs, refs = refs[: len(chunks)], refs[len(chunks) : 2 * len(chunks)], refs[2 * len(chunks) :]
    uk_ref, uv_ref, uk2_ref, uv2_ref, ok_ref, ov_ref, latt_ref, fk_ref, fv_ref, fq_ref = refs[:10]
    out_ref, keep_ref, send_ref, gk_ref, gv_ref, gl_ref = refs[10:]
    blocks = [(c, k, v, 0, k.shape[1]) for c, k, v in zip(chunks, k_refs, gp_refs)]
    gq = fq_ref[...] + head_grads(gaps_ref, q_ref, do_ref, st_refs, blocks, gk_ref, gv_ref)
    rest = fk_ref.shape[0]
    terms = [
        (latt_ref[:, :rest], (fk_ref[...], fv_ref[...])),
        (latt_ref[:, rest:], (gk_ref[...], gv_ref[...])),
    ]
    up_grads(pl.program_id(0), terms, gq, out_ref)
    add_latent(gl_ref, (gk_ref, gv_ref, uk_ref, uv_ref), (ok_ref, ov_ref, uk2_ref, uv2_ref), keep_ref, send_ref)


def turn_kernel(*refs):
    rb = refs[0].shape[0]
    for i, ref in enumerate(refs[:-1]):
        refs[-1][:, i * rb : (i + 1) * rb] = ref[...].T


def run_turn(pieces):
    rb, depth = pieces[0].shape
    return pl.pallas_call(
        turn_kernel,
        out_shape=jax.ShapeDtypeStruct((depth, rb * len(pieces)), BF16),
        compiler_params=pltpu.CompilerParams(vmem_limit_bytes=VMEM),
        name="turn",
    )(*pieces)


def part_shape(n, depth, qn, cols):
    return jax.ShapeDtypeStruct((n, depth // n + qn // n // 2, 2 * cols), BF16)


def run_whole(gaps, queries, grad_out, stats, k2, v, latt, lower, upper, pairs, held=()):
    n = len(stats)
    depth = latt.shape[0]
    rows = sum(x.shape[1] for x in k2)
    qn = queries.shape[0]
    wide = PAIR * HD
    cols = (upper - lower) * wide
    col = lambda g, *_: (0, lower + g)
    block = lambda g, *_: (lower + g, 0, 0)
    part = part_shape(n, depth, qn, cols)
    operands = (gaps, queries, grad_out, *stats, *k2, *v, latt)
    return pl.pallas_call(
        functools.partial(whole_kernel, n, len(held)),
        out_shape=(jax.ShapeDtypeStruct((rows, pairs * wide), BF16),) * 2 + (part,),
        grid_spec=pltpu.PrefetchScalarGridSpec(
            num_scalar_prefetch=1,
            grid=(upper - lower,),
            in_specs=[pl.BlockSpec((qn, wide), col)] * 2
            + [pl.BlockSpec((None, 8, qn), block)] * n
            + [pl.BlockSpec((PAIR, *x.shape[1:]), block) for x in (*k2, *v)]
            + [pl.BlockSpec(latt.shape, lambda g, *_: (0, 0))]
            + [pl.BlockSpec(memory_space=pl.ANY)] * len(held),
            out_specs=[pl.BlockSpec((rows, wide), col)] * 2
            + [pl.BlockSpec(part.shape, lambda g, *_: (0, 0, 0))],
        ),
        input_output_aliases={len(operands) + i: i for i in range(len(held))},
        compiler_params=pltpu.CompilerParams(vmem_limit_bytes=VMEM),
        cost_estimate=pl.CostEstimate(
            flops=cols * rows * 2 * (7 * qn + 2 * depth), bytes_accessed=cols * rows * 10, transcendentals=0
        ),
        name="whole",
    )(*operands, *held)


def run_split(far, gaps, queries, grad_out, stats, k2, v, chunks, up_key, up_value, other, first, pairs,
              latt=None, before=()):
    n = len(stats)
    size = k2[0].shape[1]
    depth = up_key.shape[0]
    rb = size // 2
    rows = size * len(chunks)
    qn = queries.shape[0]
    wide = PAIR * HD
    cols = pairs * wide
    span = first // pairs * wide
    own = lambda g, *_: (0, first + g)
    own3 = lambda g, *_: (first + g, 0, 0)
    out = col = lambda g, *_: (0, g)
    fixed = lambda g, *_: (0, 0)
    fixed3 = lambda g, *_: (0, 0, 0)

    def rows_of(chunk):
        if chunk == 0:
            return 0, own3
        return 1, lambda g, *_: (first + g, chunk - 1, 0)

    picked = [rows_of(c) for c in chunks]
    in_specs = [pl.BlockSpec((qn, wide), own)] * 2 + [pl.BlockSpec((None, 8, qn), own3)] * n
    in_specs += [pl.BlockSpec((PAIR, size, 2 * HD), index) for _, index in picked]
    in_specs += [pl.BlockSpec((PAIR, size, qn), index) for _, index in picked]
    in_specs += [pl.BlockSpec((depth, wide), own)] * 2 + [pl.BlockSpec((depth, span), col)] * 2
    in_specs += [pl.BlockSpec((rows, span), lambda g, *_: (0 if far else other[0].shape[0] // rows - 1, g))] * 2
    grads = (jax.ShapeDtypeStruct((rows, cols), BF16),) * 2
    sums = (jax.ShapeDtypeStruct((len(chunks), rb, depth), BF16),) * 2
    sum_specs = [pl.BlockSpec(sums[0].shape, fixed3)] * 2
    gl = pltpu.VMEM((rows, depth), F32)
    if far:
        kernel = far_kernel
        out_shape = grads + (jax.ShapeDtypeStruct((qn, cols), F32),) + sums
        out_specs = [pl.BlockSpec((rows, wide), out)] * 2 + [pl.BlockSpec((qn, wide), out)] + sum_specs
        scratch = [gl]
    else:
        kernel = near_kernel
        part = part_shape(n, depth, qn, cols)
        in_specs += [pl.BlockSpec(latt.shape, fixed)]
        in_specs += [pl.BlockSpec((before[0].shape[0], wide), out)] * 2 + [pl.BlockSpec((qn, wide), out)]
        out_shape = (part,) + sums
        out_specs = [pl.BlockSpec(part.shape, fixed3)] + sum_specs
        scratch = [pltpu.VMEM((rows, wide), BF16)] * 2
        scratch += [gl]
    return pl.pallas_call(
        functools.partial(kernel, n, chunks),
        out_shape=out_shape,
        grid_spec=pltpu.PrefetchScalarGridSpec(
            num_scalar_prefetch=1,
            grid=(pairs,),
            in_specs=in_specs,
            out_specs=out_specs,
            scratch_shapes=scratch,
        ),
        compiler_params=pltpu.CompilerParams(vmem_limit_bytes=VMEM),
        cost_estimate=pl.CostEstimate(
            flops=cols * rows * 2 * (7 * qn + 4 * depth) + first * wide * rows * 4 * depth,
            bytes_accessed=cols * rows * 10,
            transcendentals=0,
        ),
        name="far" if far else "near",
    )(gaps, queries, grad_out, *stats, *[k2[i] for i, _ in picked], *[v[i] for i, _ in picked],
      up_key, up_value, up_key, up_value, *other, *([] if far else [latt]), *before)


def after(value, *others):
    return lax.optimization_barrier((value, *others))[0]


def local(queries, grad_out, latent, up_key, up_value):
    heads = queries.shape[1] // HD
    qn = queries.shape[0]
    n = lax.axis_size("ctx")
    mates = lax.axis_size("head")
    rb, depth = latent.shape
    chunks = mates // 2
    near = 1

    firsts = [latent] + [swap(latent, "head", 2 * k) for k in range(1, chunks)]
    starts = (lax.axis_index("ctx") * mates + (lax.axis_index("head") ^ jnp.arange(mates))) * rb
    gaps = (rb * mates * n - qn - starts).astype(jnp.int32)
    k2, v, every, stats = [], [], [], None
    for which in ([0], list(range(1, chunks))):
        pieces = []
        for c in which:
            mine = firsts[c] if stats is None else after(firsts[c], stats)
            pieces += [mine, swap(mine, "head", 1)]
        one_k2, one_v, stats = run_stats(
            2 * which[0], gaps, pieces, up_key, up_value, queries, grad_out, stats
        )
        k2.append(one_k2)
        v.append(one_v)
        every += pieces
    latt = run_turn([after(every[2], stats)] + every[3:] + every[:2])
    stats = [stats] + [swap(stats, "ctx", k) for k in range(1, n)]

    pairs = heads // PAIR
    first = 3 * pairs // 4
    held, outs = (), []
    for lower, upper in ((0, first),):
        gk, gv, part = run_whole(gaps, queries, grad_out, stats, k2, v, latt, lower, upper, first, held)
        held = (gk, gv)
        outs.append(lax.all_to_all(part, "ctx", 0, 0, tiled=True))
    split = functools.partial(run_split, up_key=up_key, up_value=up_value, other=(gk, gv), first=first,
                              pairs=pairs - first, queries=queries, grad_out=grad_out, stats=stats, k2=k2, v=v)
    fk, fv, fq, far, far_away = split(True, gaps, chunks=list(range(near, chunks)))
    far = far.astype(F32) + swap(far_away, "head", 1).astype(F32)
    far = far.astype(BF16)
    part, close, close_away = split(
        False, after(gaps, far), chunks=list(range(near)), latt=latt, before=(fk, fv, fq)
    )
    outs.append(lax.all_to_all(after(part, outs[0]), "ctx", 0, 0, tiled=True))
    got = [swap(far[k], "head", 2 * (near + k)) for k in range(chunks - near)]
    close = close.astype(F32) + swap(close_away, "head", 1).astype(F32)
    grad_latent = close[0]
    *got, outs[1] = lax.optimization_barrier((*got, outs[1]))
    for x in got:
        grad_latent = grad_latent + x.astype(F32)

    sums = [functools.reduce(jnp.add, [o[k].astype(F32) for k in range(n)]) for o in outs]
    ub = depth // n
    grad_key = jnp.concatenate([s[:ub, : s.shape[1] // 2] for s in sums], axis=1)
    grad_value = jnp.concatenate([s[:ub, s.shape[1] // 2 :] for s in sums], axis=1)
    grad_q = jnp.concatenate(
        [jnp.concatenate([s[ub:, : s.shape[1] // 2], s[ub:, s.shape[1] // 2 :]], axis=0) for s in sums], axis=1
    )
    return (grad_q, grad_latent, grad_key, grad_value)


def solution(mesh):
    return jax.shard_map(
        local,
        mesh=mesh,
        in_specs=(
            P(None, "head"),
            P(None, "head"),
            P(("ctx", "head"), None),
            P(None, "head"),
            P(None, "head"),
        ),
        out_specs=(P("ctx", "head"), P(("ctx", "head"), None), P("ctx", "head"), P("ctx", "head")),
        check_vma=False,
    )
```
